32 devices in a mesh: rows: 32 (over z, y, x, core).
Axes of the slice: x: 2, y: 2, z: 4, core: 2. Of those that a mesh axis runs over, the one named last changes fastest.
Arguments:
- ham: bfloat16 [32, 10, 128, 128], P('rows'), may hold values from -0.5 to 0.5
- hpat: int32 [32, 10], replicated, may hold values from -1 to 31, as said below
- kpat: int32 [32, 30], replicated, may hold values from -1 to 31, as said below
- coefs: float32 [4], replicated, may hold values from -1 to 1
Outputs:
- density: float32 [32, 30, 128, 128], P('rows')
The draws below stay inside these ranges and needn't reach their ends.
Inputs may be any that keep to these rules, and one draw needn't show every extreme that they name: Slot 0 of row i of hpat is i; the used slots of a row name distinct block columns within 6 of i; unused slots (-1) occur only where fewer than 10 columns lie inside the grid. Slot 0 of row i of kpat is i; the used slots of a row name distinct block columns within 24 of i, from half of 30 to 30 of them (fewer only near the grid's ends); some row uses all 30 slots; unused slots hold -1.
All inputs are finite; a program needn't handle non-finite values.
Results may differ from the reference program's by a relative error of at most 0.0029.
Values may be sent and summed in bfloat16 or wider, within the bound.
A program may use at most 128 MiB of HBM per device.

```python
import jax
import jax.numpy as jnp
from jax import lax

BLK = 128
HB = 10
KB = 30
HREACH = 6
KREACH = 24
NB = 32


def choose_pattern(key, width, reach, least):
    rows = jnp.arange(NB, dtype=jnp.int32)
    span = 2 * reach + 1
    offsets = jnp.arange(span, dtype=jnp.int32) - reach
    cand = rows[:, None] + offsets[None, :]
    valid = (cand >= 0) & (cand < NB)
    keys = jax.random.split(key, NB)
    ranks = jax.vmap(lambda k: jax.random.permutation(k, span))(keys).astype(jnp.int32)
    prio = jnp.where(offsets[None, :] == 0, -1, ranks) + jnp.where(valid, 0, 2 * span)
    order = jnp.argsort(prio, axis=1, stable=True)[:, :width]
    cols = jnp.take_along_axis(cand, order, axis=1)
    live = jnp.take_along_axis(valid, order, axis=1)
    counts = jax.random.randint(jax.random.fold_in(key, 7), (NB,), least, width + 1).astype(jnp.int32)
    counts = counts.at[NB // 2].set(width)
    slots = jnp.arange(width, dtype=jnp.int32)
    return jnp.where(live & (slots[None, :] < counts[:, None]), cols, -1).astype(jnp.int32)


def nearest_pattern(key, width, reach, least):
    rows = jnp.arange(NB, dtype=jnp.int32)
    span = 2 * reach + 1
    offsets = jnp.arange(span, dtype=jnp.int32) - reach
    cand = rows[:, None] + offsets[None, :]
    valid = (cand >= 0) & (cand < NB)
    jitter = jax.random.randint(jax.random.fold_in(key, 3), (NB, span), 0, 6).astype(jnp.int32)
    score = 4 * jnp.abs(offsets)[None, :] + jitter
    score = jnp.where(offsets[None, :] == 0, -1, score) + jnp.where(valid, 0, 16 * span)
    prio = score * span + jnp.arange(span, dtype=jnp.int32)[None, :]
    order = jnp.argsort(prio, axis=1, stable=True)[:, :width]
    cols = jnp.take_along_axis(cand, order, axis=1)
    live = jnp.take_along_axis(valid, order, axis=1)
    counts = jax.random.randint(jax.random.fold_in(key, 7), (NB,), least, width + 1).astype(jnp.int32)
    counts = counts.at[NB // 2].set(width)
    slots = jnp.arange(width, dtype=jnp.int32)
    return jnp.where(live & (slots[None, :] < counts[:, None]), cols, -1).astype(jnp.int32)


def draw_hpat(key, part):
    key = jax.random.fold_in(key, 1)
    return choose_pattern(key, HB, HREACH, HB)


def draw_kpat(key, part):
    key = jax.random.fold_in(key, 2)
    return nearest_pattern(key, KB, KREACH, KB // 2)


def block_scale(own_key, shape, pieces, smallest, largest):
    level, own = 1.0, jax.random.fold_in(own_key, 6)
    for dim, shards_of in pieces:
        heights = jnp.exp(jax.random.uniform(jax.random.fold_in(own, dim), (shards_of,), jnp.float32, smallest / len(pieces), largest / len(pieces)))
        level = level * jnp.repeat(heights, shape[dim] // shards_of).reshape([-1 if axis == dim else 1 for axis in range(len(shape))])
    return level


def centred(rng, shape, deviation, most, shards=(), kind=jnp.bfloat16):
    entries = jax.random.normal(rng, shape, jnp.float32) * deviation
    if len(shards) > 0:
        entries = block_scale(rng, shape, shards, -0.22, 0.18) * entries
    return jnp.clip(entries, min=-most, max=most).astype(kind)


def setup_inputs(seed: int = 0) -> dict:
    splits = jax.random.split(jax.random.key(seed), 5)
    ham = centred(splits[0], (NB, HB, BLK, BLK), BLK ** -0.5, 0.5, ((0, 32),))
    hpat = draw_hpat(jax.random.fold_in(splits[4], 71), 0)
    kpat = draw_kpat(jax.random.fold_in(splits[4], 71), 0)
    coefs = jnp.clip(jax.random.uniform(splits[3], (4,), jnp.float32, -1.0, 1.0), -1.0, 1.0)
    return dict(ham=ham, hpat=hpat, kpat=kpat, coefs=coefs)


def gather_blocks(table, pattern, row_h, row_k):
    owner = jnp.clip(row_h, 0, NB - 1).astype(jnp.int32)
    pats = pattern[owner]
    match = (pats[:, None, :] == row_k[None, :, None]) & (row_k[None, :, None] >= 0) & (row_h[:, None, None] >= 0)
    slot = jnp.argmax(match, axis=2).astype(jnp.int32)
    found = jnp.any(match, axis=2)
    picked = table[owner[:, None], slot]
    return jnp.where(found[:, :, None, None], picked, jnp.zeros_like(picked))


def first_terms(ham, hpat, kpat, index):
    blk = ham.shape[-1]
    eye = jnp.eye(blk, dtype=jnp.float32)
    row_h = hpat[index]
    row_k = kpat[index]
    term0 = jnp.where((row_k == index)[:, None, None], eye[None], jnp.zeros((1, blk, blk), jnp.float32))
    match_one = ((row_h[None, :] == row_k[:, None]) & (row_k[:, None] >= 0)).astype(jnp.float32)
    term1 = jnp.einsum("jh,hab->jab", match_one, ham[index].astype(jnp.float32), precision=lax.Precision.HIGHEST)
    return row_h, row_k, term0, term1


def reference(ham, hpat, kpat, coefs):
    rows = jnp.arange(NB, dtype=jnp.int32)

    def second(index):
        row_h, row_k, term0, term1 = first_terms(ham, hpat, kpat, index)
        picked = gather_blocks(ham, hpat, row_h, row_k)
        prod = jnp.einsum("hab,hjbc->jac", ham[index].astype(jnp.float32), picked.astype(jnp.float32))
        return (2.0 * prod - term0).astype(jnp.bfloat16)

    term2_all = lax.map(second, rows)

    def third(index):
        row_h, row_k, term0, term1 = first_terms(ham, hpat, kpat, index)
        picked = gather_blocks(term2_all, kpat, row_h, row_k)
        prod = jnp.einsum("hab,hjbc->jac", ham[index].astype(jnp.float32), picked.astype(jnp.float32))
        term3 = 2.0 * prod - term1
        return coefs[0] * term0 + coefs[1] * term1 + coefs[2] * term2_all[index].astype(jnp.float32) + coefs[3] * term3

    return lax.map(third, rows)
```

```python
import functools

import jax
import jax.numpy as jnp
from jax import lax
from jax.experimental import pallas as pl
from jax.experimental.pallas import tpu as pltpu
from jax.sharding import PartitionSpec as P

R = 6
SPAN = 2 * R + 1
WIDE = 4 * R + 1
COLS = 6 * R + 1
TALL = SPAN + 2
MESH = pl.DeviceIdType.MESH


def kernel(count, coefs, inv, tidx, slot1, diag, ham, out, *scratch):
    w = scratch[:WIDE]
    band, t2, send, fsend, recv = scratch[WIDE:]
    b = ham.shape[-1]
    kb = out.shape[0]
    mid = 2 * R
    me = lax.axis_index("rows")
    delta = 1 - 2 * lax.rem(me, 2)
    sib = me + delta

    def inside(row):
        return (row >= 0) & (row < count)

    barrier = pltpu.get_barrier_semaphore()
    pl.semaphore_signal(barrier, inc=1, device_id=(sib,), device_id_type=MESH)
    steps = [s * sign for s in range(1, R + 1) for sign in (1, -1)]
    for s in steps:
        @pl.when(inside(me + 2 * s))
        def _(s=s):
            pl.semaphore_signal(barrier, inc=1, device_id=(me + 2 * s,), device_id_type=MESH)
    peers = 1 + sum(jnp.where(inside(me + 2 * s), 1, 0) for s in steps)
    pl.semaphore_wait(barrier, peers)

    def direct(s):
        return pltpu.make_async_remote_copy(
            src_ref=ham, dst_ref=w[mid - 2 * s], send_sem=send.at[s + R], recv_sem=recv.at[mid - 2 * s],
            device_id=(me + 2 * s,), device_id_type=MESH)

    def arrived(r):
        pltpu.make_async_remote_copy(
            src_ref=ham, dst_ref=w[r], send_sem=send.at[0], recv_sem=recv.at[r],
            device_id=(sib,), device_id_type=MESH).wait_recv()

    def passed(s, d):
        r = mid + 2 * s - d
        return pltpu.make_async_remote_copy(
            src_ref=ham if s == 0 else w[mid + 2 * s], dst_ref=w[r], send_sem=fsend.at[s + R],
            recv_sem=recv.at[r], device_id=(sib,), device_id_type=MESH)

    def pass_on(s, act):
        for d in (1, -1):
            if 0 <= mid + 2 * s - d < WIDE:
                @pl.when((delta == d) & inside(me + 2 * s))
                def _(d=d):
                    act(passed(s, d))

    pass_on(0, lambda c: c.start())
    for s in steps:
        @pl.when(inside(me + 2 * s))
        def _(s=s):
            direct(s).start()

    zero = jnp.zeros((b, b), jnp.bfloat16)
    for q in range(COLS):
        band[q, 0:b, :] = zero
        band[q, (TALL - 1) * b:, :] = zero

    def spread(r):
        src = ham if r == mid else w[r]
        for d in range(SPAN):
            slot = inv[r * SPAN + d]
            block = src[jnp.maximum(slot, 0)]
            band[r + d, (SPAN - d) * b:(SPAN + 1 - d) * b, :] = jnp.where(slot >= 0, block, zero)

    def fetch(r):
        if r % 2 == 0:
            s = (r - mid) // 2
            @pl.when(inside(me + 2 * s))
            def _():
                arrived(r)
            pass_on(s, lambda c: c.start())
        else:
            @pl.when(inside(me + r - mid))
            def _():
                arrived(r)

    ident = jnp.where(
        lax.broadcasted_iota(jnp.int32, (b, b), 0) == lax.broadcasted_iota(jnp.int32, (b, b), 1), 1.0, 0.0)

    def second(t):
        left = jnp.concatenate(
            [band[t + R + d, (SPAN - d) * b:(SPAN + 1 - d) * b, :] for d in range(SPAN)], axis=1)
        for e in range(0, WIDE, 2):
            es = [e] if e + 1 == WIDE else [e, e + 1]
            lo, hi = max(0, e - SPAN + 1), min(SPAN - 1, es[-1])
            right = jnp.concatenate(
                [band[t + x, (lo - x + SPAN) * b:(hi - x + SPAN + 1) * b, :] for x in es], axis=1)
            prod = jnp.dot(left[:, lo * b:(hi + 1) * b], right, preferred_element_type=jnp.float32)
            for n, x in enumerate(es):
                got = 2.0 * prod[:, n * b:(n + 1) * b]
                if x == 2 * R:
                    got = got - ident
                t2[t * WIDE + x] = got.astype(jnp.bfloat16)

    spread(mid)
    for r in sorted((x for x in range(R, 3 * R + 1) if x != mid and x % 2 == 0), key=lambda x: abs(x - mid)):
        fetch(r)
        spread(r)
    for r in sorted((x for x in range(R, 3 * R + 1) if x % 2), key=lambda x: abs(x - mid)):
        fetch(r)
        spread(r)
    second(R)
    for u in range(1, R + 1):
        if u % 2:
            for r in (R - u - 1, 3 * R + u + 1, R - u, 3 * R + u):
                fetch(r)
        for r in (R - u, 3 * R + u):
            spread(r)

        @pl.loop(0, 2)
        def _(j, u=u):
            second(R - u + 2 * u * j)

    left = jnp.concatenate(
        [band[2 * R + d, (SPAN - d) * b:(SPAN + 1 - d) * b, :] for d in range(SPAN)], axis=1)
    c0, c1, c2, c3 = coefs[0], coefs[1], coefs[2], coefs[3]

    def column(g, t):
        e = tidx[g * SPAN + t]
        return jnp.where(e >= 0, t2[t * WIDE + jnp.maximum(e, 0)], zero)

    @pl.loop(0, kb // 2)
    def _(p):
        gs = [2 * p, 2 * p + 1]
        right = jnp.concatenate(
            [jnp.concatenate([column(g, t) for t in range(SPAN)], axis=0) for g in gs], axis=1)
        prod = jnp.dot(left, right, preferred_element_type=jnp.float32)
        for n, g in enumerate(gs):
            slot = slot1[g]
            one = jnp.where(slot >= 0, ham[jnp.maximum(slot, 0)], zero).astype(jnp.float32)
            two = column(g, R).astype(jnp.float32)
            start = jnp.where(diag[g] > 0, ident, 0.0)
            out[g] = c0 * start + c1 * one + c2 * two + c3 * (2.0 * prod[:, n * b:(n + 1) * b] - one)

    for s in steps:
        @pl.when(inside(me + 2 * s))
        def _(s=s):
            direct(s).wait_send()
    for s in [0] + steps:
        pass_on(s, lambda c: c.wait_send())


def body(ham, hpat, kpat, coefs):
    own = lax.axis_index("rows")
    count = lax.axis_size("rows")
    _, hb, b, _ = ham.shape
    kb = kpat.shape[1]
    hrows = lax.dynamic_slice(
        jnp.pad(hpat, ((2 * R, 2 * R), (0, 0)), constant_values=-1), (own, 0), (WIDE, hb))
    cols = own - 3 * R + jnp.arange(WIDE)[:, None] + jnp.arange(SPAN)[None, :]
    hit = (hrows[:, None, :] == cols[:, :, None]) & (cols >= 0)[:, :, None]
    inv = jnp.max(jnp.where(hit, jnp.arange(hb), -1), axis=2).reshape(-1)
    krows = lax.dynamic_slice(
        jnp.pad(kpat, ((R, R), (0, 0)), constant_values=-1), (own, 0), (SPAN, kb))
    row_k, row_h = krows[R], hrows[2 * R]
    far = row_k[:, None] - (own - R + jnp.arange(SPAN))[None, :] + 2 * R
    held = jnp.any(krows[None, :, :] == row_k[:, None, None], axis=2)
    tidx = jnp.where(held & (row_k >= 0)[:, None] & (far >= 0) & (far < WIDE), far, -1).reshape(-1)
    one = (row_h[None, :] == row_k[:, None]) & (row_k >= 0)[:, None]
    slot1 = jnp.max(jnp.where(one, jnp.arange(hb), -1), axis=1)
    diag = (row_k == own).astype(jnp.int32)
    smem = pl.BlockSpec(memory_space=pltpu.SMEM)
    vmem = pl.BlockSpec(memory_space=pltpu.VMEM)
    row = pltpu.VMEM((hb, b, b), jnp.bfloat16)
    got = pl.pallas_call(
        functools.partial(kernel, count),
        out_shape=jax.ShapeDtypeStruct((kb, b, b), jnp.float32),
        in_specs=[smem] * 5 + [vmem],
        out_specs=vmem,
        scratch_shapes=[row] * WIDE + [
            pltpu.VMEM((COLS, TALL * b, b), jnp.bfloat16),
            pltpu.VMEM((SPAN * WIDE, b, b), jnp.bfloat16),
            pltpu.SemaphoreType.DMA((SPAN,)),
            pltpu.SemaphoreType.DMA((SPAN,)),
            pltpu.SemaphoreType.DMA((WIDE,)),
        ],
        compiler_params=pltpu.CompilerParams(
            collective_id=0, has_side_effects=True, vmem_limit_bytes=56 * 1024 * 1024),
        cost_estimate=pl.CostEstimate(flops=10**10, bytes_accessed=10**7, transcendentals=0),
    )(coefs, inv, tidx, slot1, diag, ham[0])
    return got[None]


def solution(mesh):
    in_specs = (P("rows", None, None, None), P(), P(), P())
    out_specs = P("rows", None, None, None)
    return jax.shard_map(body, mesh=mesh, in_specs=in_specs, out_specs=out_specs, check_vma=False)
```

```python
import functools

import jax
import jax.numpy as jnp
from jax import lax
from jax.experimental import pallas as pl
from jax.experimental.pallas import tpu as pltpu
from jax.sharding import PartitionSpec as P

R = 6
SPAN = 2 * R + 1
WIDE = 4 * R + 1
COLS = 6 * R + 1
TALL = SPAN + 2
MESH = pl.DeviceIdType.MESH


def kernel(count, coefs, inv, tidx, slot1, diag, ham, out, *scratch):
    w = scratch[:WIDE]
    band, t2, send, fsend, recv = scratch[WIDE:]
    b = ham.shape[-1]
    kb = out.shape[0]
    mid = 2 * R
    me = lax.axis_index("rows")
    delta = 1 - 2 * lax.rem(me, 2)
    sib = me + delta

    def inside(row):
        return (row >= 0) & (row < count)

    chip = lax.div(me, 2)
    place = lax.rem(chip, 4)
    hb = ham.shape[0]
    cut = hb // 2
    halves = [(0, cut), (cut, hb - cut)]

    def inside(row):
        return (row >= 0) & (row < count)

    barrier = pltpu.get_barrier_semaphore()
    near = [me + 2 * (1 - 2 * lax.rem(place, 2)), me + 4 * (1 - 2 * lax.div(place, 2)), me + 8, me - 8]
    pl.semaphore_signal(barrier, inc=1, device_id=(sib,), device_id_type=MESH)
    for other in near:
        @pl.when(inside(other))
        def _(other=other):
            pl.semaphore_signal(barrier, inc=1, device_id=(other,), device_id_type=MESH)
    peers = 1 + sum(jnp.where(inside(other), 1, 0) for other in near)
    pl.semaphore_wait(barrier, peers)

    def part(ref, n):
        return ref.at[pl.ds(*halves[n])]

    def row_ref(s):
        return ham if s == 0 else w[mid + 2 * s]

    def relay(s, n, link, step):
        r = mid + 2 * (s - step)
        return pltpu.make_async_remote_copy(
            src_ref=part(row_ref(s), n), dst_ref=part(w[r], n), send_sem=send.at[(s + R) * 8 + link * 2 + n],
            recv_sem=recv.at[2 * r + n], device_id=(me + 2 * step,), device_id_type=MESH)

    def arrived(r, n):
        pltpu.make_async_remote_copy(
            src_ref=part(ham, n), dst_ref=part(w[r], n), send_sem=fsend.at[0], recv_sem=recv.at[2 * r + n],
            device_id=(sib,), device_id_type=MESH).wait_recv()

    def pass_on(s, n, act):
        for d in (1, -1):
            r = mid + 2 * s - d
            if 0 <= r < WIDE:
                @pl.when(delta == d)
                def _(r=r):
                    act(pltpu.make_async_remote_copy(
                        src_ref=part(row_ref(s), n), dst_ref=part(w[r], n), send_sem=fsend.at[2 * (s + R) + n],
                        recv_sem=recv.at[2 * r + n], device_id=(sib,), device_id_type=MESH))

    def route(o, s, n):
        if s == 0:
            return 0, 0
        z, p = (o + s) // 4, (o + s) % 4
        x, y = (o ^ 1) - o, (o ^ 2) - o
        if z == 0:
            if p == o ^ 3:
                return (x if n == 0 else y), 2
            return s, 1
        sign = 1 if z > 0 else -1
        if abs(z) == 1 and p in (o ^ 1, o ^ 2):
            step = x if p == o ^ 1 else y
            return step, 2
        step = 4 * sign
        if s == step:
            return step, 1
        return step, route(o, s - step, n)[1] + 1

    def sends(o, s, n):
        out_steps = []
        for link, step in enumerate(((o ^ 1) - o, (o ^ 2) - o, 4, -4)):
            t = s - step
            if t != 0 and abs(t) <= R and route((o + step) % 4, t, n)[0] == -step:
                out_steps.append((link, step))
        return out_steps

    def plan(o):
        keys = [(route(o, s, n)[1], n, abs(s), s) for s in range(-R, R + 1) for n in (0, 1)]
        return [(h, s, n) for h, n, _, s in sorted(keys)]

    def ship(o, s, n, act):
        for link, step in sends(o, s, n):
            @pl.when(inside(me + 2 * step))
            def _(link=link, step=step):
                act(relay(s, n, link, step))
        pass_on(s, n, act)

    def each_place(f):
        for o in range(4):
            @pl.when(place == o)
            def _(o=o):
                f(o)

    def level(hops):
        def go(o):
            for h, s, n in plan(o):
                if h in hops:
                    @pl.when(inside(me + 2 * s))
                    def _(s=s, n=n):
                        if h > 0:
                            arrived(mid + 2 * s, n)
                        ship(o, s, n, lambda c: c.start())
        each_place(go)

    level((0,))

    zero = jnp.zeros((b, b), jnp.bfloat16)
    for q in range(COLS):
        band[q, 0:b, :] = zero
        band[q, (TALL - 1) * b:, :] = zero

    def spread(r):
        src = ham if r == mid else w[r]
        for d in range(SPAN):
            slot = inv[r * SPAN + d]
            block = src[jnp.maximum(slot, 0)]
            band[r + d, (SPAN - d) * b:(SPAN + 1 - d) * b, :] = jnp.where(slot >= 0, block, zero)

    def fetch(r):
        @pl.when(inside(me + r - mid))
        def _():
            for n in (0, 1):
                arrived(r, n)

    ident = jnp.where(
        lax.broadcasted_iota(jnp.int32, (b, b), 0) == lax.broadcasted_iota(jnp.int32, (b, b), 1), 1.0, 0.0)

    def second(t):
        left = jnp.concatenate(
            [band[t + R + d, (SPAN - d) * b:(SPAN + 1 - d) * b, :] for d in range(SPAN)], axis=1)
        for e in range(0, WIDE, 2):
            es = [e] if e + 1 == WIDE else [e, e + 1]
            lo, hi = max(0, e - SPAN + 1), min(SPAN - 1, es[-1])
            right = jnp.concatenate(
                [band[t + x, (lo - x + SPAN) * b:(hi - x + SPAN + 1) * b, :] for x in es], axis=1)
            prod = jnp.dot(left[:, lo * b:(hi + 1) * b], right, preferred_element_type=jnp.float32)
            for n, x in enumerate(es):
                got = 2.0 * prod[:, n * b:(n + 1) * b]
                if x == 2 * R:
                    got = got - ident
                t2[t * WIDE + x] = got.astype(jnp.bfloat16)

    spread(mid)
    level((1,))
    level((2,))
    level((3, 4))
    for r in range(WIDE):
        if r % 2:
            fetch(r)
        if r != mid:
            spread(r)

    @pl.loop(0, SPAN)
    def _(t):
        second(t)

    left = jnp.concatenate(
        [band[2 * R + d, (SPAN - d) * b:(SPAN + 1 - d) * b, :] for d in range(SPAN)], axis=1)
    c0, c1, c2, c3 = coefs[0], coefs[1], coefs[2], coefs[3]

    def column(g, t):
        e = tidx[g * SPAN + t]
        return jnp.where(e >= 0, t2[t * WIDE + jnp.maximum(e, 0)], zero)

    @pl.loop(0, kb // 2)
    def _(p):
        gs = [2 * p, 2 * p + 1]
        right = jnp.concatenate(
            [jnp.concatenate([column(g, t) for t in range(SPAN)], axis=0) for g in gs], axis=1)
        prod = jnp.dot(left, right, preferred_element_type=jnp.float32)
        for n, g in enumerate(gs):
            slot = slot1[g]
            one = jnp.where(slot >= 0, ham[jnp.maximum(slot, 0)], zero).astype(jnp.float32)
            two = column(g, R).astype(jnp.float32)
            start = jnp.where(diag[g] > 0, ident, 0.0)
            out[g] = c0 * start + c1 * one + c2 * two + c3 * (2.0 * prod[:, n * b:(n + 1) * b] - one)

    def drain(o):
        for _, s, n in plan(o):
            @pl.when(inside(me + 2 * s))
            def _(s=s, n=n):
                ship(o, s, n, lambda c: c.wait_send())

    each_place(drain)


def body(ham, hpat, kpat, coefs):
    own = lax.axis_index("rows")
    count = lax.axis_size("rows")
    _, hb, b, _ = ham.shape
    kb = kpat.shape[1]
    hrows = lax.dynamic_slice(
        jnp.pad(hpat, ((2 * R, 2 * R), (0, 0)), constant_values=-1), (own, 0), (WIDE, hb))
    cols = own - 3 * R + jnp.arange(WIDE)[:, None] + jnp.arange(SPAN)[None, :]
    hit = (hrows[:, None, :] == cols[:, :, None]) & (cols >= 0)[:, :, None]
    inv = jnp.max(jnp.where(hit, jnp.arange(hb), -1), axis=2).reshape(-1)
    krows = lax.dynamic_slice(
        jnp.pad(kpat, ((R, R), (0, 0)), constant_values=-1), (own, 0), (SPAN, kb))
    row_k, row_h = krows[R], hrows[2 * R]
    far = row_k[:, None] - (own - R + jnp.arange(SPAN))[None, :] + 2 * R
    held = jnp.any(krows[None, :, :] == row_k[:, None, None], axis=2)
    tidx = jnp.where(held & (row_k >= 0)[:, None] & (far >= 0) & (far < WIDE), far, -1).reshape(-1)
    one = (row_h[None, :] == row_k[:, None]) & (row_k >= 0)[:, None]
    slot1 = jnp.max(jnp.where(one, jnp.arange(hb), -1), axis=1)
    diag = (row_k == own).astype(jnp.int32)
    smem = pl.BlockSpec(memory_space=pltpu.SMEM)
    vmem = pl.BlockSpec(memory_space=pltpu.VMEM)
    row = pltpu.VMEM((hb, b, b), jnp.bfloat16)
    got = pl.pallas_call(
        functools.partial(kernel, count),
        out_shape=jax.ShapeDtypeStruct((kb, b, b), jnp.float32),
        in_specs=[smem] * 5 + [vmem],
        out_specs=vmem,
        scratch_shapes=[row] * WIDE + [
            pltpu.VMEM((COLS, TALL * b, b), jnp.bfloat16),
            pltpu.VMEM((SPAN * WIDE, b, b), jnp.bfloat16),
            pltpu.SemaphoreType.DMA((SPAN * 8,)),
            pltpu.SemaphoreType.DMA((SPAN * 2,)),
            pltpu.SemaphoreType.DMA((WIDE * 2,)),
        ],
        compiler_params=pltpu.CompilerParams(
            collective_id=0, has_side_effects=True, vmem_limit_bytes=56 * 1024 * 1024),
        cost_estimate=pl.CostEstimate(flops=10**10, bytes_accessed=10**7, transcendentals=0),
    )(coefs, inv, tidx, slot1, diag, ham[0])
    return got[None]


def solution(mesh):
    in_specs = (P("rows", None, None, None), P(), P(), P())
    out_specs = P("rows", None, None, None)
    return jax.shard_map(body, mesh=mesh, in_specs=in_specs, out_specs=out_specs, check_vma=False)
```

```python
import functools

import jax
import jax.numpy as jnp
from jax import lax
from jax.experimental import pallas as pl
from jax.experimental.pallas import tpu as pltpu
from jax.sharding import PartitionSpec as P

R = 6
SPAN = 2 * R + 1
WIDE = 4 * R + 1
COLS = 6 * R + 1
TALL = SPAN + 2
MESH = pl.DeviceIdType.MESH


def kernel(count, coefs, hpat, kpat, ham, out, *scratch):
    w = scratch[:WIDE]
    band, t2, slots, used, send, fsend, recv = scratch[WIDE:]
    b = ham.shape[-1]
    kb = out.shape[0]
    mid = 2 * R
    me = lax.axis_index("rows")
    delta = 1 - 2 * lax.rem(me, 2)
    sib = me + delta

    def inside(row):
        return (row >= 0) & (row < count)

    chip = lax.div(me, 2)
    place = lax.rem(chip, 4)
    hb = ham.shape[0]
    cut = hb // 2
    halves = [(0, cut), (cut, hb - cut)]

    def inside(row):
        return (row >= 0) & (row < count)

    barrier = pltpu.get_barrier_semaphore()
    near = [me + 2 * (1 - 2 * lax.rem(place, 2)), me + 4 * (1 - 2 * lax.div(place, 2)), me + 8, me - 8]
    pl.semaphore_signal(barrier, inc=1, device_id=(sib,), device_id_type=MESH)
    for other in near:
        @pl.when(inside(other))
        def _(other=other):
            pl.semaphore_signal(barrier, inc=1, device_id=(other,), device_id_type=MESH)
    peers = 1 + sum(jnp.where(inside(other), 1, 0) for other in near)
    pl.semaphore_wait(barrier, peers)

    def part(ref, n):
        return ref.at[pl.ds(*halves[n])]

    def row_ref(s):
        return ham if s == 0 else w[mid + 2 * s]

    def relay(s, n, link, step):
        r = mid + 2 * (s - step)
        return pltpu.make_async_remote_copy(
            src_ref=part(row_ref(s), n), dst_ref=part(w[r], n), send_sem=send.at[(s + R) * 8 + link * 2 + n],
            recv_sem=recv.at[2 * r + n], device_id=(me + 2 * step,), device_id_type=MESH)

    def arrived(r, n):
        pltpu.make_async_remote_copy(
            src_ref=part(ham, n), dst_ref=part(w[r], n), send_sem=fsend.at[0], recv_sem=recv.at[2 * r + n],
            device_id=(sib,), device_id_type=MESH).wait_recv()

    def pass_on(s, n, act):
        for d in (1, -1):
            r = mid + 2 * s - d
            if 0 <= r < WIDE:
                @pl.when(delta == d)
                def _(r=r):
                    act(pltpu.make_async_remote_copy(
                        src_ref=part(row_ref(s), n), dst_ref=part(w[r], n), send_sem=fsend.at[2 * (s + R) + n],
                        recv_sem=recv.at[2 * r + n], device_id=(sib,), device_id_type=MESH))

    def route(o, s, n):
        if s == 0:
            return 0, 0
        z, p = (o + s) // 4, (o + s) % 4
        x, y = (o ^ 1) - o, (o ^ 2) - o
        if z == 0:
            if p == o ^ 3:
                return (x if n == 0 else y), 2
            return s, 1
        sign = 1 if z > 0 else -1
        flat = 1 if o in (0, 1) else -1
        if o in (0, 3) and p == o ^ 3 and z == -flat and n == 1:
            return y, route(o ^ 2, s - y, n)[1] + 1
        if o in (0, 3) and p == o ^ 3 and z == -2 * flat and n == 0:
            return x, route(o ^ 1, s - x, n)[1] + 1
        if abs(z) == 1 and p in (o ^ 1, o ^ 2):
            if z == flat and (o in (0, 3) or n == (0 if p == o ^ 1 else 1)):
                return 4 * sign, route(o, s - 4 * sign, n)[1] + 1
            return (x if p == o ^ 1 else y), 2
        step = 4 * sign
        if s == step:
            return step, 1
        return step, route(o, s - step, n)[1] + 1

    def sends(o, s, n):
        out_steps = []
        for link, step in enumerate(((o ^ 1) - o, (o ^ 2) - o, 4, -4)):
            t = s - step
            if t != 0 and abs(t) <= R and route((o + step) % 4, t, n)[0] == -step:
                out_steps.append((link, step))
        return out_steps

    def plan(o):
        keys = [(route(o, s, n)[1], n, abs(s), s) for s in range(-R, R + 1) for n in (0, 1)]
        return [(h, s, n) for h, n, _, s in sorted(keys)]

    def ship(o, s, n, act):
        for link, step in sends(o, s, n):
            @pl.when(inside(me + 2 * step))
            def _(link=link, step=step):
                act(relay(s, n, link, step))
        pass_on(s, n, act)

    def each_place(f):
        for o in range(4):
            @pl.when(place == o)
            def _(o=o):
                f(o)

    def level(hops):
        def go(o):
            for h, s, n in plan(o):
                if h in hops:
                    @pl.when(inside(me + 2 * s))
                    def _(s=s, n=n):
                        if h > 0:
                            arrived(mid + 2 * s, n)
                        ship(o, s, n, lambda c: c.start())
        each_place(go)

    level((0,))

    zero = jnp.zeros((b, b), jnp.bfloat16)
    for q in range(COLS):
        band[q, 0:b, :] = zero
        band[q, (TALL - 1) * b:, :] = zero

    def find(named, col):
        slot = jnp.int32(-1)
        for h in range(hb):
            slot = jnp.where(named[h] == col, h, slot)
        return slot

    @pl.loop(0, WIDE)
    def _(r):
        row = me + r - mid
        named = [hpat[jnp.clip(row, 0, count - 1), h] for h in range(hb)]
        for d in range(SPAN):
            col = row - R + d
            slots[r * SPAN + d] = jnp.where(inside(row) & (col >= 0), find(named, col), -1)

    @pl.loop(0, SPAN)
    def _(t):
        row = me - R + t
        word = jnp.int32(0)
        for u in range(kb):
            col = kpat[jnp.clip(row, 0, count - 1), u]
            e = col - row + 2 * R
            ok = (col >= 0) & (e >= 0) & (e < WIDE) & inside(row)
            word = word | jnp.where(ok, jnp.left_shift(1, jnp.clip(e, 0, WIDE - 1)), 0)
        used[t] = word

    def spread(r):
        src = ham if r == mid else w[r]
        for d in range(SPAN):
            slot = slots[r * SPAN + d]
            block = src[jnp.maximum(slot, 0)]
            band[r + d, (SPAN - d) * b:(SPAN + 1 - d) * b, :] = jnp.where(slot >= 0, block, zero)

    def fetch(r):
        @pl.when(inside(me + r - mid))
        def _():
            for n in (0, 1):
                arrived(r, n)

    ident = jnp.where(
        lax.broadcasted_iota(jnp.int32, (b, b), 0) == lax.broadcasted_iota(jnp.int32, (b, b), 1), 1.0, 0.0)

    def second(h):
        t = jnp.clip(hpat[me, h] - me + R, 0, SPAN - 1)
        left = jnp.concatenate(
            [band[t + R + d, (SPAN - d) * b:(SPAN + 1 - d) * b, :] for d in range(SPAN)], axis=1)
        for e in range(0, WIDE, 2):
            es = [e] if e + 1 == WIDE else [e, e + 1]
            lo, hi = max(0, e - SPAN + 1), min(SPAN - 1, es[-1])
            right = jnp.concatenate(
                [band[t + x, (lo - x + SPAN) * b:(hi - x + SPAN + 1) * b, :] for x in es], axis=1)
            prod = jnp.dot(left[:, lo * b:(hi + 1) * b], right, preferred_element_type=jnp.float32)
            for n, x in enumerate(es):
                got = 2.0 * prod[:, n * b:(n + 1) * b]
                if x == 2 * R:
                    got = got - ident
                t2[h * WIDE + x] = got.astype(jnp.bfloat16)

    spread(mid)
    level((1,))
    level((2,))

    def soon(r):
        got = False
        for o in range(4):
            for d in (1, -1):
                if r % 2 or d == 1:
                    s = (r - mid - (d if r % 2 else 0)) // 2
                    if abs(s) <= R and max(route(o, s, 0)[1], route(o, s, 1)[1]) <= 2:
                        here = place == o
                        got = got | ((here & (delta == d)) if r % 2 else here)
        return got

    def settle(r):
        if r % 2:
            fetch(r)
        spread(r)

    others = [r for r in range(WIDE) if r != mid]
    for r in others:
        @pl.when(soon(r))
        def _(r=r):
            settle(r)
    level((3, 4, 5))
    for r in others:
        @pl.when(jnp.logical_not(soon(r)))
        def _(r=r):
            settle(r)

    @pl.loop(0, hb)
    def _(h):
        second(h)

    left = jnp.concatenate([ham[h] for h in range(hb)], axis=1)
    c0, c1, c2, c3 = coefs[0], coefs[1], coefs[2], coefs[3]

    named = [hpat[me, h] for h in range(hb)]
    words = [used[jnp.clip(named[h] - me + R, 0, SPAN - 1)] for h in range(hb)]

    def column(col, h):
        e = col - named[h] + 2 * R
        at = jnp.clip(e, 0, WIDE - 1)
        ok = (named[h] >= 0) & (col >= 0) & (e == at) & ((jnp.right_shift(words[h], at) & 1) == 1)
        return jnp.where(ok, t2[h * WIDE + at], zero)

    @pl.loop(0, kb // 2)
    def _(p):
        gs = [2 * p, 2 * p + 1]
        cols = [kpat[me, g] for g in gs]
        right = jnp.concatenate(
            [jnp.concatenate([column(col, h) for h in range(hb)], axis=0) for col in cols], axis=1)
        prod = jnp.dot(left, right, preferred_element_type=jnp.float32)
        for n, g in enumerate(gs):
            col = cols[n]
            slot = jnp.where(col >= 0, find(named, col), -1)
            one = jnp.where(slot >= 0, ham[jnp.maximum(slot, 0)], zero).astype(jnp.float32)
            two = column(col, 0).astype(jnp.float32)
            start = jnp.where(col == me, ident, 0.0)
            out[g] = c0 * start + c1 * one + c2 * two + c3 * (2.0 * prod[:, n * b:(n + 1) * b] - one)

    def drain(o):
        for _, s, n in plan(o):
            @pl.when(inside(me + 2 * s))
            def _(s=s, n=n):
                ship(o, s, n, lambda c: c.wait_send())

    each_place(drain)


def body(ham, hpat, kpat, coefs):
    count = lax.axis_size("rows")
    _, hb, b, _ = ham.shape
    kb = kpat.shape[1]
    smem = pl.BlockSpec(memory_space=pltpu.SMEM)
    vmem = pl.BlockSpec(memory_space=pltpu.VMEM)
    row = pltpu.VMEM((hb, b, b), jnp.bfloat16)
    got = pl.pallas_call(
        functools.partial(kernel, count),
        out_shape=jax.ShapeDtypeStruct((kb, b, b), jnp.float32),
        in_specs=[smem] * 3 + [vmem],
        out_specs=vmem,
        scratch_shapes=[row] * WIDE + [
            pltpu.VMEM((COLS, TALL * b, b), jnp.bfloat16),
            pltpu.VMEM((hb * WIDE, b, b), jnp.bfloat16),
            pltpu.SMEM((WIDE * SPAN,), jnp.int32),
            pltpu.SMEM((SPAN,), jnp.int32),
            pltpu.SemaphoreType.DMA((SPAN * 8,)),
            pltpu.SemaphoreType.DMA((SPAN * 2,)),
            pltpu.SemaphoreType.DMA((WIDE * 2,)),
        ],
        compiler_params=pltpu.CompilerParams(
            collective_id=0, has_side_effects=True, vmem_limit_bytes=56 * 1024 * 1024),
        cost_estimate=pl.CostEstimate(flops=10**10, bytes_accessed=10**7, transcendentals=0),
    )(coefs, hpat, kpat, ham[0])
    return got[None]


def solution(mesh):
    in_specs = (P("rows", None, None, None), P(), P(), P())
    out_specs = P("rows", None, None, None)
    return jax.shard_map(body, mesh=mesh, in_specs=in_specs, out_specs=out_specs, check_vma=False)
```

```python
import functools

import jax
import jax.numpy as jnp
from jax import lax
from jax.experimental import pallas as pl
from jax.experimental.pallas import tpu as pltpu
from jax.sharding import PartitionSpec as P

R = 6
SPAN = 2 * R + 1
WIDE = 4 * R + 1
COLS = 6 * R + 1
TALL = SPAN + 2
MESH = pl.DeviceIdType.MESH


def kernel(count, coefs, hpat, kpat, ham, out, *scratch):
    w = scratch[:WIDE]
    band, t2, slots, used, send, fsend, recv = scratch[WIDE:]
    b = ham.shape[-1]
    kb = out.shape[0]
    mid = 2 * R
    me = lax.axis_index("rows")
    delta = 1 - 2 * lax.rem(me, 2)
    sib = me + delta

    def inside(row):
        return (row >= 0) & (row < count)

    chip = lax.div(me, 2)
    place = lax.rem(chip, 4)
    hb = ham.shape[0]
    cut = hb // 2
    halves = [(0, cut), (cut, hb - cut)]

    def inside(row):
        return (row >= 0) & (row < count)

    barrier = pltpu.get_barrier_semaphore()
    near = [me + 2 * (1 - 2 * lax.rem(place, 2)), me + 4 * (1 - 2 * lax.div(place, 2)), me + 8, me - 8]
    pl.semaphore_signal(barrier, inc=1, device_id=(sib,), device_id_type=MESH)
    for other in near:
        @pl.when(inside(other))
        def _(other=other):
            pl.semaphore_signal(barrier, inc=1, device_id=(other,), device_id_type=MESH)
    peers = 1 + sum(jnp.where(inside(other), 1, 0) for other in near)
    pl.semaphore_wait(barrier, peers)

    def part(ref, n):
        return ref.at[pl.ds(*halves[n])]

    def row_ref(s):
        return ham if s == 0 else w[mid + 2 * s]

    def relay(s, n, link, step):
        r = mid + 2 * (s - step)
        return pltpu.make_async_remote_copy(
            src_ref=part(row_ref(s), n), dst_ref=part(w[r], n), send_sem=send.at[(s + R) * 8 + link * 2 + n],
            recv_sem=recv.at[2 * r + n], device_id=(me + 2 * step,), device_id_type=MESH)

    def arrived(r, n):
        pltpu.make_async_remote_copy(
            src_ref=part(ham, n), dst_ref=part(w[r], n), send_sem=fsend.at[0], recv_sem=recv.at[2 * r + n],
            device_id=(sib,), device_id_type=MESH).wait_recv()

    def pass_on(s, n, act):
        for d in (1, -1):
            r = mid + 2 * s - d
            if 0 <= r < WIDE:
                @pl.when(delta == d)
                def _(r=r):
                    act(pltpu.make_async_remote_copy(
                        src_ref=part(row_ref(s), n), dst_ref=part(w[r], n), send_sem=fsend.at[2 * (s + R) + n],
                        recv_sem=recv.at[2 * r + n], device_id=(sib,), device_id_type=MESH))

    def route(o, s, n):
        if s == 0:
            return 0, 0
        z, p = (o + s) // 4, (o + s) % 4
        x, y = (o ^ 1) - o, (o ^ 2) - o
        if z == 0:
            if p == o ^ 3:
                return (x if n == 0 else y), 2
            return s, 1
        sign = 1 if z > 0 else -1
        flat = 1 if o in (0, 1) else -1
        if o in (0, 3) and p == o ^ 3 and z == -flat and n == 1:
            return y, route(o ^ 2, s - y, n)[1] + 1
        if o in (0, 3) and p == o ^ 3 and z == -2 * flat and n == 0:
            return x, route(o ^ 1, s - x, n)[1] + 1
        if abs(z) == 1 and p in (o ^ 1, o ^ 2):
            if z == flat and (o in (0, 3) or n == (0 if p == o ^ 1 else 1)):
                return 4 * sign, route(o, s - 4 * sign, n)[1] + 1
            return (x if p == o ^ 1 else y), 2
        step = 4 * sign
        if s == step:
            return step, 1
        return step, route(o, s - step, n)[1] + 1

    def sends(o, s, n):
        out_steps = []
        for link, step in enumerate(((o ^ 1) - o, (o ^ 2) - o, 4, -4)):
            t = s - step
            if t != 0 and abs(t) <= R and route((o + step) % 4, t, n)[0] == -step:
                out_steps.append((link, step))
        return out_steps

    def plan(o):
        keys = [(route(o, s, n)[1], n, abs(s), s) for s in range(-R, R + 1) for n in (0, 1)]
        return [(h, s, n) for h, n, _, s in sorted(keys)]

    def ship(o, s, n, act):
        for link, step in sends(o, s, n):
            @pl.when(inside(me + 2 * step))
            def _(link=link, step=step):
                act(relay(s, n, link, step))
        pass_on(s, n, act)

    def each_place(f):
        for o in range(4):
            @pl.when(place == o)
            def _(o=o):
                f(o)

    def level(hops):
        def go(o):
            for h, s, n in plan(o):
                if h in hops:
                    @pl.when(inside(me + 2 * s))
                    def _(s=s, n=n):
                        if h > 0:
                            arrived(mid + 2 * s, n)
                        ship(o, s, n, lambda c: c.start())
        each_place(go)

    level((0,))

    zero = jnp.zeros((b, b), jnp.bfloat16)
    for q in range(COLS):
        band[q, 0:b, :] = zero
        band[q, (TALL - 1) * b:, :] = zero

    def find(named, col):
        slot = jnp.int32(-1)
        for h in range(hb):
            slot = jnp.where(named[h] == col, h, slot)
        return slot

    @pl.loop(0, WIDE)
    def _(r):
        row = me + r - mid
        named = [hpat[jnp.clip(row, 0, count - 1), h] for h in range(hb)]
        for d in range(SPAN):
            col = row - R + d
            slots[r * SPAN + d] = jnp.where(inside(row) & (col >= 0), find(named, col), -1)

    @pl.loop(0, SPAN)
    def _(t):
        row = me - R + t
        word = jnp.int32(0)
        for u in range(kb):
            col = kpat[jnp.clip(row, 0, count - 1), u]
            e = col - row + 2 * R
            ok = (col >= 0) & (e >= 0) & (e < WIDE) & inside(row)
            word = word | jnp.where(ok, jnp.left_shift(1, jnp.clip(e, 0, WIDE - 1)), 0)
        used[t] = word

    def spread(r):
        src = ham if r == mid else w[r]
        for d in range(SPAN):
            slot = slots[r * SPAN + d]
            block = src[jnp.maximum(slot, 0)]
            band[r + d, (SPAN - d) * b:(SPAN + 1 - d) * b, :] = jnp.where(slot >= 0, block, zero)

    def fetch(r):
        @pl.when(inside(me + r - mid))
        def _():
            for n in (0, 1):
                arrived(r, n)

    ident = jnp.where(
        lax.broadcasted_iota(jnp.int32, (b, b), 0) == lax.broadcasted_iota(jnp.int32, (b, b), 1), 1.0, 0.0)

    def second(h):
        t = jnp.clip(hpat[me, h] - me + R, 0, SPAN - 1)
        left = jnp.concatenate(
            [band[t + R + d, (SPAN - d) * b:(SPAN + 1 - d) * b, :] for d in range(SPAN)], axis=1)
        for e in range(0, WIDE, 2):
            es = [e] if e + 1 == WIDE else [e, e + 1]
            lo, hi = max(0, e - SPAN + 1), min(SPAN - 1, es[-1])
            right = jnp.concatenate(
                [band[t + x, (lo - x + SPAN) * b:(hi - x + SPAN + 1) * b, :] for x in es], axis=1)
            prod = jnp.dot(left[:, lo * b:(hi + 1) * b], right, preferred_element_type=jnp.float32)
            for n, x in enumerate(es):
                got = 2.0 * prod[:, n * b:(n + 1) * b]
                if x == 2 * R:
                    got = got - ident
                t2[h * WIDE + x] = got.astype(jnp.bfloat16)

    spread(mid)
    level((1,))
    level((2,))

    def soon(r):
        got = False
        for o in range(4):
            for d in (1, -1):
                if r % 2 or d == 1:
                    s = (r - mid - (d if r % 2 else 0)) // 2
                    if abs(s) <= R and max(route(o, s, 0)[1], route(o, s, 1)[1]) <= 2:
                        here = place == o
                        got = got | ((here & (delta == d)) if r % 2 else here)
        return got

    def settle(r):
        if r % 2:
            fetch(r)
        spread(r)

    others = [r for r in range(WIDE) if r != mid]
    for r in others:
        @pl.when(soon(r))
        def _(r=r):
            settle(r)
    level((3, 4, 5))
    for r in others:
        @pl.when(jnp.logical_not(soon(r)))
        def _(r=r):
            settle(r)

    @pl.loop(0, hb)
    def _(h):
        second(h)

    left = jnp.concatenate([ham[h] for h in range(hb)], axis=1)
    c0, c1, c2, c3 = coefs[0], coefs[1], coefs[2], coefs[3]

    named = [hpat[me, h] for h in range(hb)]
    words = [used[jnp.clip(named[h] - me + R, 0, SPAN - 1)] for h in range(hb)]

    def column(col, h):
        e = col - named[h] + 2 * R
        at = jnp.clip(e, 0, WIDE - 1)
        ok = (named[h] >= 0) & (col >= 0) & (e == at) & ((jnp.right_shift(words[h], at) & 1) == 1)
        return jnp.where(ok, t2[h * WIDE + at], zero)

    def third(p):
        gs = [2 * p, 2 * p + 1]
        cols = [kpat[me, g] for g in gs]
        right = jnp.concatenate(
            [jnp.concatenate([column(col, h) for h in range(hb)], axis=0) for col in cols], axis=1)
        prod = jnp.dot(left, right, preferred_element_type=jnp.float32)
        for n, g in enumerate(gs):
            col = cols[n]
            slot = jnp.where(col >= 0, find(named, col), -1)
            one = jnp.where(slot >= 0, ham[jnp.maximum(slot, 0)], zero).astype(jnp.float32)
            two = column(col, 0).astype(jnp.float32)
            start = jnp.where(col == me, ident, 0.0)
            out[g] = c0 * start + c1 * one + c2 * two + c3 * (2.0 * prod[:, n * b:(n + 1) * b] - one)

    pairs = kb // 2
    group = 3 if pairs % 3 == 0 else 1

    @pl.loop(0, pairs // group)
    def _(p):
        for n in range(group):
            third(p * group + n)

    def drain(o):
        for _, s, n in plan(o):
            @pl.when(inside(me + 2 * s))
            def _(s=s, n=n):
                ship(o, s, n, lambda c: c.wait_send())

    each_place(drain)


def body(ham, hpat, kpat, coefs):
    count = lax.axis_size("rows")
    _, hb, b, _ = ham.shape
    kb = kpat.shape[1]
    smem = pl.BlockSpec(memory_space=pltpu.SMEM)
    vmem = pl.BlockSpec(memory_space=pltpu.VMEM)
    row = pltpu.VMEM((hb, b, b), jnp.bfloat16)
    got = pl.pallas_call(
        functools.partial(kernel, count),
        out_shape=jax.ShapeDtypeStruct((kb, b, b), jnp.float32),
        in_specs=[smem] * 3 + [vmem],
        out_specs=vmem,
        scratch_shapes=[row] * WIDE + [
            pltpu.VMEM((COLS, TALL * b, b), jnp.bfloat16),
            pltpu.VMEM((hb * WIDE, b, b), jnp.bfloat16),
            pltpu.SMEM((WIDE * SPAN,), jnp.int32),
            pltpu.SMEM((SPAN,), jnp.int32),
            pltpu.SemaphoreType.DMA((SPAN * 8,)),
            pltpu.SemaphoreType.DMA((SPAN * 2,)),
            pltpu.SemaphoreType.DMA((WIDE * 2,)),
        ],
        compiler_params=pltpu.CompilerParams(
            collective_id=0, has_side_effects=True, vmem_limit_bytes=56 * 1024 * 1024),
        cost_estimate=pl.CostEstimate(flops=10**10, bytes_accessed=10**7, transcendentals=0),
    )(coefs, hpat, kpat, ham[0])
    return got[None]


def solution(mesh):
    in_specs = (P("rows", None, None, None), P(), P(), P())
    out_specs = P("rows", None, None, None)
    return jax.shard_map(body, mesh=mesh, in_specs=in_specs, out_specs=out_specs, check_vma=False)
```
